32 devices in a mesh: groups: 2 (over y), dp: 4 (over z), tensor: 4 (over x, core).
Axes of the slice: x: 2, y: 2, z: 4, core: 2. Of those that a mesh axis runs over, the one named last changes fastest.
Arguments:
- hidden: bfloat16 [1024, 29568], P(('groups', 'dp'), 'tensor'), parts along dimension 0, may hold values from -6 to 6
- down_matrix: bfloat16 [29568, 8192], P('tensor', 'dp'), may hold values from -0.03125 to 0.03125
- adapter_first: bfloat16 [29568, 128], P('tensor'), may hold values from -0.03125 to 0.03125
- adapter_second: bfloat16 [128, 8192], replicated, may hold values from -0.25 to 0.25
- scoring_matrix: float32 [8192], P('dp'), may hold values from -0.6 to 0.6
- lengths: int32 [16], P('groups'), parts along dimension 0, may hold values from 1 to 64, as said below
- group_labels: int32 [16], P('groups'), parts along dimension 0, may hold values from 0 to 1, as said below
Outputs:
- policy_out: bfloat16 [1024, 8192], P(('groups', 'tensor'), 'dp'), parts along dimension 0
- reference_out: bfloat16 [1024, 8192], P(('groups', 'tensor'), 'dp'), parts along dimension 0
- advantage: float32 [16], P('groups'), parts along dimension 0
The draws below stay inside these ranges and needn't reach their ends.
There are 2 independent parts, one for each index of `groups`. The reference program is written for one: setup_inputs(seed, part) draws one part's arguments, and reference() takes and returns one part's arrays. A program takes and returns all parts, laid end to end along the dimension named above; an argument that names none is the same for every part. Nothing has to cross between parts.
Inputs may be any that keep to these rules, and one draw needn't show every extreme that they name: `lengths`: some response has length 64. `group_labels`: every group number is held by exactly 4 responses.
All inputs are finite; a program needn't handle non-finite values.
Results may differ from the reference program's by a relative error of at most 0.0051.
Values may be sent and summed in bfloat16 or wider, within the bound.
A program may use at most 128 MiB of HBM per device.

```python
import jax
import jax.numpy as jnp
from jax import lax

MODEL_WIDTH = 8192
HIDDEN_UNITS = 29568
ADAPTER_RANK = 128
GSIZE = 4
TOKENS = 512
SEQS = 8
SLOT = 64


def draw_lengths(key, part):
    key = jax.random.fold_in(key, 11)
    key_lens, key_full = jax.random.split(key)
    drawn = jax.random.randint(key_lens, (SEQS,), 1, SLOT + 1)
    full_at = jax.random.randint(key_full, (), 0, SEQS)
    return jnp.where(jnp.arange(SEQS) == full_at, SLOT, drawn).astype(jnp.int32)


def draw_group_labels(key, part):
    key = jax.random.fold_in(key, 23)
    shuffled = jax.random.permutation(key, SEQS)
    return (shuffled // GSIZE).astype(jnp.int32)


def steps_of(own_key, dims, cuts, low, largest):
    factor_of, own = 1.0, jax.random.fold_in(own_key, 6)
    for axis_at, blocks in cuts:
        heights = jnp.exp(jax.random.uniform(jax.random.fold_in(own, axis_at), (blocks,), jnp.float32, low / len(cuts), largest / len(cuts)))
        factor_of = factor_of * jnp.repeat(heights, dims[axis_at] // blocks).reshape([-1 if axis == axis_at else 1 for axis in range(len(dims))])
    return factor_of


def scatter_about(stream_key, dims, scale, bound, cuts=(), held_as=jnp.bfloat16):
    entries = jax.random.normal(stream_key, dims, jnp.float32) * scale
    if len(cuts) > 0:
        entries = steps_of(stream_key, dims, cuts, -0.22, 0.18) * entries
    return jnp.clip(entries, min=-bound, max=bound).astype(held_as)


def setup_inputs(seed: int = 0, part: int = 0) -> dict:
    key_list = jax.random.split(jax.random.key(seed), 8)
    part_splits = jax.random.split(jax.random.fold_in(key_list[7], part), 8)
    return {
        "hidden": scatter_about(part_splits[0], (TOKENS, HIDDEN_UNITS), 1.0, 6.0, ((0, 4), (1, 4))),
        "down_matrix": scatter_about(key_list[1], (HIDDEN_UNITS, MODEL_WIDTH), HIDDEN_UNITS ** -0.5, 0.03125, ((0, 4), (1, 4))),
        "adapter_first": scatter_about(key_list[2], (HIDDEN_UNITS, ADAPTER_RANK), HIDDEN_UNITS ** -0.5, 0.03125, ((0, 4),)),
        "adapter_second": scatter_about(key_list[3], (ADAPTER_RANK, MODEL_WIDTH), (4 * ADAPTER_RANK) ** -0.5, 0.25),
        "scoring_matrix": scatter_about(key_list[4], (MODEL_WIDTH,), 0.1, 0.6, ((0, 4),), jnp.float32),
        "lengths": draw_lengths(jax.random.fold_in(jax.random.fold_in(key_list[7], part), 71), part),
        "group_labels": draw_group_labels(jax.random.fold_in(jax.random.fold_in(key_list[7], part), 71), part),
    }


ADAPTER_SCALE = 2.0


def reference(hidden, down_matrix, adapter_first, adapter_second, scoring_matrix, lengths, group_labels):
    base_sum = jnp.dot(hidden, down_matrix, preferred_element_type=jnp.float32)
    rank_output = jnp.dot(hidden, adapter_first, preferred_element_type=jnp.float32)
    adapter_factors = ADAPTER_SCALE * jnp.dot(rank_output, adapter_second.astype(jnp.float32), precision=lax.Precision.HIGHEST)
    row_ids = jnp.arange(TOKENS, dtype=jnp.int32)
    row_lengths = jnp.repeat(lengths, SLOT)
    is_valid = ((row_ids % SLOT) < row_lengths)[:, None]
    policy_out = jnp.where(is_valid, base_sum + adapter_factors, 0.0).astype(jnp.bfloat16)
    reference_out = jnp.where(is_valid, base_sum, 0.0).astype(jnp.bfloat16)
    token_scores = jnp.dot(policy_out.astype(jnp.float32), scoring_matrix, precision=lax.Precision.HIGHEST)
    seq_score = token_scores.reshape(SEQS, SLOT).sum(axis=1) / lengths.astype(jnp.float32)
    same_group = (group_labels[:, None] == group_labels[None, :]).astype(jnp.float32)
    group_mean = jnp.dot(same_group, seq_score, precision=lax.Precision.HIGHEST) / GSIZE
    return policy_out, reference_out, seq_score - group_mean
```

```python
import functools

import jax
import jax.numpy as jnp
from jax import lax
from jax.experimental import pallas as pl
from jax.experimental.pallas import tpu as pltpu
from jax.sharding import PartitionSpec as P

GSIZE = 4
ADAPTER_SCALE = 2.0
MESH = pl.DeviceIdType.MESH

CHUNK = 16
BLOCK = 64
SLOTS = 4
LAG = 2
TILES = BLOCK // CHUNK
WIDE = 1024


def place(onehot, src, start, count, dst):
    width = src.shape[1]
    for at in range(0, width, WIDE):
        cols = pl.ds(at, min(WIDE, width - at))
        picked = jnp.dot(
            onehot, src[pl.ds(start, count), cols], preferred_element_type=jnp.float32
        )
        dst[:, cols] = picked.astype(dst.dtype)


def stream_kernel(
    n, steps, count_ref, pack_ref, own_ref, down_ref, first_ref, part_ref,
    from_low, from_high, down, first, own, out_up, out_down,
    load_sem, send_up, send_down, recv_up, recv_down,
):
    me = lax.axis_index("dp")
    rows = own_ref.shape[0]
    columns = down_ref.shape[1]
    load_down = pltpu.make_async_copy(down_ref, down, load_sem.at[0])
    load_first = pltpu.make_async_copy(first_ref, first, load_sem.at[1])
    load_own = pltpu.make_async_copy(own_ref, own, load_sem.at[2])
    load_own.start()
    load_down.start()
    load_first.start()

    barrier = pltpu.get_barrier_semaphore()

    for near in (lax.rem(me + 1, n), lax.rem(me + n - 1, n)):
        pl.semaphore_signal(barrier, inc=1, device_id={"dp": near}, device_id_type=MESH)

    load_own.wait()
    place(pack_ref[...], own, 0, rows, from_low.at[pl.ds(0, rows)])
    place(pack_ref[...], own, 0, rows, from_high.at[pl.ds(0, rows)])

    def clear(ref, before):
        start = pl.multiple_of(rows + rows * before, rows)
        ref[pl.ds(start, rows), :] = jnp.zeros((rows, ref.shape[1]), ref.dtype)

    @pl.when(me < n - 1)
    def _():
        clear(from_low, me)

    @pl.when(me > 0)
    def _():
        clear(from_high, n - 1 - me)

    part_ref[...] = jnp.zeros_like(part_ref)

    pl.semaphore_wait(barrier, 2)
    count = count_ref[0]

    def copy_of(source, out, send, recv, target, step):
        slot = lax.rem(step, SLOTS)
        start = pl.multiple_of(rows + step * CHUNK, CHUNK)
        return pltpu.make_async_remote_copy(
            src_ref=out.at[slot],
            dst_ref=source.at[pl.ds(start, CHUNK)],
            send_sem=send.at[slot],
            recv_sem=recv.at[step],
            device_id={"dp": target},
            device_id_type=MESH,
        )

    up = (from_low, out_up, send_up, recv_up)
    low = (from_high, out_down, send_down, recv_down)

    def advance(direction, target, before, step):
        source, out, send, recv = direction
        copy = copy_of(source, out, send, recv, target, step)

        @pl.when(step * CHUNK < rows * before)
        def _():
            copy.wait_recv()

        @pl.when((before < n - 1) & (step * CHUNK < rows * (before + 1)))
        def _():
            @pl.when(step >= SLOTS)
            def _():
                copy.wait_send()

            line = step * CHUNK + lax.broadcasted_iota(jnp.int32, (CHUNK, CHUNK + rows), 0)
            entry = step * CHUNK + lax.broadcasted_iota(jnp.int32, (CHUNK, CHUNK + rows), 1)
            wanted = jnp.where(line < count, line, line + (rows - count))
            onehot = jnp.where(entry == wanted, 1.0, 0.0).astype(jnp.bfloat16)
            start = pl.multiple_of(step * CHUNK, CHUNK)
            place(onehot, source, start, CHUNK + rows, out.at[lax.rem(step, SLOTS)])
            copy.start()

    tile = columns // TILES

    def multiply(source, start, put, size, j):
        block = pl.ds(pl.multiple_of(start, BLOCK), size)
        lines = pl.ds(pl.multiple_of(put, BLOCK), size)
        cols = pl.ds(pl.multiple_of(j * tile, tile), tile)
        part_ref[lines, cols] = jnp.dot(
            source[block, :], down[:, cols], preferred_element_type=jnp.float32
        ).astype(part_ref.dtype)

        @pl.when(j == 0)
        def _():
            part_ref[lines, pl.ds(columns, first.shape[1])] = jnp.dot(
                source[block, :], first[...], preferred_element_type=jnp.float32
            ).astype(part_ref.dtype)

    to_up = lax.rem(me + 1, n)
    to_low = lax.rem(me + n - 1, n)
    above = n - 1 - me

    def turn(u, _):
        up_step = u - LAG * me
        low_step = u - LAG * above

        @pl.when((up_step >= 0) & (up_step < steps))
        def _():
            advance(up, to_up, me, up_step)

        @pl.when((low_step >= 0) & (low_step < steps))
        def _():
            advance(low, to_low, above, low_step)

        @pl.when(u == 2)
        def _():
            load_down.wait()
            load_first.wait()

        @pl.when((u >= 2) & (u < 2 + TILES))
        def _():
            multiply(from_low, 0, 0, rows, u - 2)

        def behind(source, step, before, put):
            late = step - TILES
            at = lax.div(late, TILES) * BLOCK

            @pl.when((late >= 0) & (late < steps) & (at < rows * before))
            def _():
                multiply(source, rows + at, put + at, BLOCK, lax.rem(late, TILES))

        behind(from_low, up_step, me, rows)
        behind(from_high, low_step, above, rows + rows * me)
        return 0

    lax.fori_loop(0, steps + TILES + LAG * (n - 1), turn, 0)

    for slot in range(SLOTS):
        @pl.when(me < n - 1)
        def _():
            copy_of(*up, to_up, slot).wait_send()

        @pl.when(above < n - 1)
        def _():
            copy_of(*low, to_low, slot).wait_send()


def stream_multiply(n, steps, ident, count, pack, hidden, down_matrix, adapter_first):
    rows, depth = hidden.shape
    columns, rank = down_matrix.shape[1], adapter_first.shape[1]
    vmem = pl.BlockSpec(memory_space=pltpu.VMEM)
    anywhere = pl.BlockSpec(memory_space=pl.ANY)
    return pl.pallas_call(
        functools.partial(stream_kernel, n, steps),
        out_shape=jax.ShapeDtypeStruct((rows * n, columns + rank), jnp.bfloat16),
        in_specs=[pl.BlockSpec(memory_space=pltpu.SMEM), vmem, anywhere, anywhere, anywhere],
        out_specs=vmem,
        scratch_shapes=[
            pltpu.VMEM((rows * n, depth), jnp.bfloat16),
            pltpu.VMEM((rows * n, depth), jnp.bfloat16),
            pltpu.VMEM(down_matrix.shape, jnp.bfloat16),
            pltpu.VMEM(adapter_first.shape, jnp.bfloat16),
            pltpu.VMEM((rows, depth), jnp.bfloat16),
            pltpu.VMEM((SLOTS, CHUNK, depth), jnp.bfloat16),
            pltpu.VMEM((SLOTS, CHUNK, depth), jnp.bfloat16),
            pltpu.SemaphoreType.DMA((3,)),
            pltpu.SemaphoreType.DMA((SLOTS,)),
            pltpu.SemaphoreType.DMA((SLOTS,)),
            pltpu.SemaphoreType.DMA((steps,)),
            pltpu.SemaphoreType.DMA((steps,)),
        ],
        compiler_params=pltpu.CompilerParams(
            collective_id=ident, has_side_effects=True, vmem_limit_bytes=62 * 2**20
        ),
        cost_estimate=pl.CostEstimate(
            flops=2 * rows * n * depth * columns,
            bytes_accessed=2 * depth * columns,
            transcendentals=0,
        ),
        name=f"stream_{steps}",
    )(count, pack, hidden, down_matrix, adapter_first)


def reduce_kernel(n, terms_ref, sum_ref, from_core, from_chip, out, send_1, recv_1, send_2, recv_2):
    me = lax.axis_index("tensor")
    core = lax.rem(me, 2)
    chip = lax.div(me, 2)
    chips = n // 2
    mate = me + 1 - 2 * core
    rows = sum_ref.shape[0]

    barrier = pltpu.get_barrier_semaphore()
    pl.semaphore_signal(barrier, inc=1, device_id={"tensor": mate}, device_id_type=MESH)
    for far in range(1, chips):
        there = lax.rem(chip + far, chips) * 2 + core
        pl.semaphore_signal(barrier, inc=1, device_id={"tensor": there}, device_id_type=MESH)
    pl.semaphore_wait(barrier, chips)

    swaps = []
    for far in [*range(1, chips), 0]:
        owner_chip = lax.rem(chip + far, chips)
        swap = pltpu.make_async_remote_copy(
            src_ref=terms_ref.at[owner_chip * 2 + 1 - core],
            dst_ref=from_core.at[far],
            send_sem=send_1.at[far],
            recv_sem=recv_1.at[far],
            device_id={"tensor": mate},
            device_id_type=MESH,
        )
        swap.start()
        swaps.append((far, owner_chip, swap))

    moves = []
    for far, owner_chip, swap in swaps:
        swap.wait_recv()
        mine = owner_chip * 2 + core

        def both(i, mine=mine, far=far):
            lines = pl.ds(pl.multiple_of(i * 16, 16), 16)
            term = terms_ref[mine, lines, :].astype(jnp.float32)
            return lines, term + from_core[far, lines, :].astype(jnp.float32)

        if far > 0:
            def lines_out(i, _, both=both, far=far):
                lines, total = both(i)
                out[far - 1, lines, :] = total.astype(out.dtype)
                return 0

            lax.fori_loop(0, rows // 16, lines_out, 0)
            move = pltpu.make_async_remote_copy(
                src_ref=out.at[far - 1],
                dst_ref=from_chip.at[far - 1],
                send_sem=send_2.at[far - 1],
                recv_sem=recv_2.at[far - 1],
                device_id={"tensor": mine},
                device_id_type=MESH,
            )
            move.start()
            moves.append(move)
        else:
            def lines_own(i, _, both=both):
                lines, total = both(i)
                sum_ref[lines, :] = total
                return 0

            lax.fori_loop(0, rows // 16, lines_own, 0)

    for far, move in enumerate(moves):
        move.wait_recv()

        def lines_in(i, _, far=far):
            lines = pl.ds(pl.multiple_of(i * 16, 16), 16)
            sum_ref[lines, :] += from_chip[far, lines, :].astype(jnp.float32)
            return 0

        lax.fori_loop(0, rows // 16, lines_in, 0)

    for _, _, swap in swaps:
        swap.wait_send()
    for move in moves:
        move.wait_send()


def reduce_blocks(n, ident, terms):
    chips = n // 2
    block = terms.shape[1:]
    vmem = pl.BlockSpec(memory_space=pltpu.VMEM)
    return pl.pallas_call(
        functools.partial(reduce_kernel, n),
        out_shape=jax.ShapeDtypeStruct(block, jnp.float32),
        in_specs=[vmem],
        out_specs=vmem,
        scratch_shapes=[
            pltpu.VMEM((chips, *block), jnp.bfloat16),
            pltpu.VMEM((chips - 1, *block), jnp.bfloat16),
            pltpu.VMEM((chips - 1, *block), jnp.bfloat16),
            pltpu.SemaphoreType.DMA((chips,)),
            pltpu.SemaphoreType.DMA((chips,)),
            pltpu.SemaphoreType.DMA((chips - 1,)),
            pltpu.SemaphoreType.DMA((chips - 1,)),
        ],
        compiler_params=pltpu.CompilerParams(
            collective_id=ident, has_side_effects=True, vmem_limit_bytes=40 * 2**20
        ),
        name="reduce_blocks",
    )(terms)


def body(hidden, down_matrix, adapter_first, adapter_second, scoring_matrix, lengths, group_labels):
    n_tensor = lax.axis_size("tensor")
    tp_index = lax.axis_index("tensor")
    n = lax.axis_size("dp")
    me = lax.axis_index("dp")
    rows = hidden.shape[0]
    output_columns = down_matrix.shape[1]
    all_rows = rows * n
    row_block = all_rows // n_tensor
    n_seqs = lengths.shape[0]
    slot_rows = all_rows // n_seqs
    seqs_block = row_block // slot_rows
    own_seqs = rows // slot_rows

    by_source = lengths.reshape(n, own_seqs)
    counts = by_source.sum(axis=1)
    before_seq = (jnp.cumsum(by_source, axis=1) - by_source).reshape(n_seqs)
    in_slot = jnp.arange(all_rows, dtype=jnp.int32) % slot_rows
    token_valid = in_slot < jnp.repeat(lengths, slot_rows)
    place_in_source = jnp.repeat(before_seq, slot_rows) + in_slot

    own_place = lax.dynamic_slice_in_dim(place_in_source, me * rows, rows, 0)
    own_valid = lax.dynamic_slice_in_dim(token_valid, me * rows, rows, 0)
    line = jnp.arange(rows, dtype=jnp.int32)[:, None]
    pack = ((own_place[None, :] == line) & own_valid[None, :]).astype(jnp.bfloat16)
    own_count = lax.dynamic_slice_in_dim(counts, me, 1, 0)

    longest = jnp.maximum(counts[:-1].sum(), counts[1:].sum())
    longest = lax.pmax(longest, "groups")
    full = rows * (n - 1) // CHUNK
    per = BLOCK // CHUNK
    choices = sorted({-(-full * part // (6 * per)) * per for part in (2, 3, 4, 5, 6)})
    limits = jnp.array([c * CHUNK for c in choices[:-1]], jnp.int32)
    chosen = (longest > limits).sum().astype(jnp.int32)
    parts = lax.switch(
        chosen,
        [functools.partial(stream_multiply, n, c, i) for i, c in enumerate(choices)],
        own_count, pack, hidden, down_matrix, adapter_first,
    )

    total = jnp.cumsum(counts)
    source = jnp.arange(n, dtype=jnp.int32)
    start = total - counts
    from_low = start[me] - total
    from_high = start - total[me]
    base_row = jnp.where(
        source == me, 0, jnp.where(source < me, rows + from_low, rows + rows * me + from_high)
    )
    token_row = jnp.repeat(base_row, rows) + place_in_source
    spread = (
        (token_row[:, None] == jnp.arange(all_rows, dtype=jnp.int32)[None, :])
        & token_valid[:, None]
    ).astype(jnp.bfloat16)
    terms = jnp.dot(spread, parts, preferred_element_type=jnp.float32).astype(jnp.bfloat16)
    summed = reduce_blocks(n_tensor, len(choices), terms.reshape(n_tensor, row_block, -1))

    base_sum = summed[:, :output_columns]
    rank_sum = summed[:, output_columns:]
    second_columns = lax.dynamic_slice_in_dim(
        adapter_second, me * output_columns, output_columns, 1
    ).astype(jnp.float32)
    policy_sum = base_sum + ADAPTER_SCALE * jnp.dot(
        rank_sum, second_columns, precision=lax.Precision.HIGHEST
    )
    block_lengths = lax.dynamic_slice_in_dim(lengths, tp_index * seqs_block, seqs_block, 0)
    row_lengths = jnp.repeat(block_lengths, slot_rows)
    is_valid = ((jnp.arange(row_block, dtype=jnp.int32) % slot_rows) < row_lengths)[:, None]
    policy_out = jnp.where(is_valid, policy_sum, 0.0).astype(jnp.bfloat16)
    reference_out = jnp.where(is_valid, base_sum, 0.0).astype(jnp.bfloat16)
    token_scores = (policy_out.astype(jnp.float32) * scoring_matrix[None, :]).sum(axis=1)
    seq_partial = token_scores.reshape(seqs_block, slot_rows).sum(axis=1)
    in_place = lax.dynamic_update_slice_in_dim(
        jnp.zeros((n_seqs,), jnp.float32), seq_partial, tp_index * seqs_block, 0
    )
    every_seq = lax.psum(in_place, ("dp", "tensor"))
    seq_score = every_seq / lengths.astype(jnp.float32)
    same_group = (group_labels[:, None] == group_labels[None, :]).astype(jnp.float32)
    group_mean = jnp.dot(same_group, seq_score, precision=lax.Precision.HIGHEST) / GSIZE
    return (policy_out, reference_out, seq_score - group_mean)


def solution(mesh):
    return jax.shard_map(
        body,
        mesh=mesh,
        in_specs=(
            P(("groups", "dp"), "tensor"),
            P("tensor", "dp"),
            P("tensor", None),
            P(),
            P("dp"),
            P("groups"),
            P("groups"),
        ),
        out_specs=(P(("groups", "tensor"), "dp"), P(("groups", "tensor"), "dp"), P("groups")),
        check_vma=False,
    )
```

```python
import functools

import jax
import jax.numpy as jnp
from jax import lax
from jax.experimental import pallas as pl
from jax.experimental.pallas import tpu as pltpu
from jax.sharding import PartitionSpec as P

GSIZE = 4
ADAPTER_SCALE = 2.0
MESH = pl.DeviceIdType.MESH

CHUNK = 16
BLOCK = 64
SLOTS = 4
LAG = 2
TILES = BLOCK // CHUNK
WIDE = 1024


def place(onehot, src, start, count, dst):
    width = src.shape[1]
    for at in range(0, width, WIDE):
        cols = pl.ds(at, min(WIDE, width - at))
        picked = jnp.dot(
            onehot, src[pl.ds(start, count), cols], preferred_element_type=jnp.float32
        )
        dst[:, cols] = picked.astype(dst.dtype)


def stream_kernel(
    n, steps, count_ref, pack_ref, own_ref, down_ref, first_ref, part_ref,
    from_low, from_high, down, first, own, out_up, out_down,
    load_sem, send_up, send_down, recv_up, recv_down,
):
    me = lax.axis_index("dp")
    rows = own_ref.shape[0]
    columns = down_ref.shape[1]
    load_down = pltpu.make_async_copy(down_ref, down, load_sem.at[0])
    load_first = pltpu.make_async_copy(first_ref, first, load_sem.at[1])
    load_own = pltpu.make_async_copy(own_ref, own, load_sem.at[2])
    load_own.start()
    load_down.start()
    load_first.start()

    barrier = pltpu.get_barrier_semaphore()

    for near in (lax.rem(me + 1, n), lax.rem(me + n - 1, n)):
        pl.semaphore_signal(barrier, inc=1, device_id={"dp": near}, device_id_type=MESH)

    load_own.wait()
    place(pack_ref[...], own, 0, rows, from_low.at[pl.ds(0, rows)])
    place(pack_ref[...], own, 0, rows, from_high.at[pl.ds(0, rows)])

    def clear(ref, before):
        start = pl.multiple_of(rows + rows * before, rows)
        ref[pl.ds(start, rows), :] = jnp.zeros((rows, ref.shape[1]), ref.dtype)

    @pl.when(me < n - 1)
    def _():
        clear(from_low, me)

    @pl.when(me > 0)
    def _():
        clear(from_high, n - 1 - me)

    part_ref[...] = jnp.zeros_like(part_ref)

    pl.semaphore_wait(barrier, 2)
    whole_steps = -(-steps // TILES) * TILES
    if whole_steps > steps:
        rest = pl.ds(rows + steps * CHUNK, (whole_steps - steps) * CHUNK)
        from_low[rest, :] = jnp.zeros((rest.size, from_low.shape[1]), from_low.dtype)
        from_high[rest, :] = jnp.zeros((rest.size, from_high.shape[1]), from_high.dtype)

    count = count_ref[0]

    def copy_of(source, out, send, recv, target, step):
        slot = lax.rem(step, SLOTS)
        start = pl.multiple_of(rows + step * CHUNK, CHUNK)
        return pltpu.make_async_remote_copy(
            src_ref=out.at[slot],
            dst_ref=source.at[pl.ds(start, CHUNK)],
            send_sem=send.at[slot],
            recv_sem=recv.at[step],
            device_id={"dp": target},
            device_id_type=MESH,
        )

    up = (from_low, out_up, send_up, recv_up)
    low = (from_high, out_down, send_down, recv_down)

    def advance(direction, target, before, step):
        source, out, send, recv = direction
        copy = copy_of(source, out, send, recv, target, step)

        @pl.when(step * CHUNK < rows * before)
        def _():
            copy.wait_recv()

        @pl.when((before < n - 1) & (step * CHUNK < rows * (before + 1)))
        def _():
            @pl.when(step >= SLOTS)
            def _():
                copy.wait_send()

            line = step * CHUNK + lax.broadcasted_iota(jnp.int32, (CHUNK, CHUNK + rows), 0)
            entry = step * CHUNK + lax.broadcasted_iota(jnp.int32, (CHUNK, CHUNK + rows), 1)
            wanted = jnp.where(line < count, line, line + (rows - count))
            onehot = jnp.where(entry == wanted, 1.0, 0.0).astype(jnp.bfloat16)
            start = pl.multiple_of(step * CHUNK, CHUNK)
            place(onehot, source, start, CHUNK + rows, out.at[lax.rem(step, SLOTS)])
            copy.start()

    tile = columns // TILES

    def multiply(source, start, put, size, j):
        block = pl.ds(pl.multiple_of(start, BLOCK), size)
        lines = pl.ds(pl.multiple_of(put, BLOCK), size)
        cols = pl.ds(pl.multiple_of(j * tile, tile), tile)
        part_ref[lines, cols] = jnp.dot(
            source[block, :], down[:, cols], preferred_element_type=jnp.float32
        ).astype(part_ref.dtype)

        @pl.when(j == 0)
        def _():
            part_ref[lines, pl.ds(columns, first.shape[1])] = jnp.dot(
                source[block, :], first[...], preferred_element_type=jnp.float32
            ).astype(part_ref.dtype)

    to_up = lax.rem(me + 1, n)
    to_low = lax.rem(me + n - 1, n)
    above = n - 1 - me

    def turn(u, _):
        up_step = u - LAG * me
        low_step = u - LAG * above

        @pl.when((up_step >= 0) & (up_step < steps))
        def _():
            advance(up, to_up, me, up_step)

        @pl.when((low_step >= 0) & (low_step < steps))
        def _():
            advance(low, to_low, above, low_step)

        @pl.when(u == 2)
        def _():
            load_down.wait()
            load_first.wait()

        @pl.when((u >= 2) & (u < 2 + TILES))
        def _():
            multiply(from_low, 0, 0, rows, u - 2)

        def behind(source, step, before, put):
            late = step - TILES
            at = lax.div(late, TILES) * BLOCK

            @pl.when((late >= 0) & (late < whole_steps) & (at < rows * before))
            def _():
                multiply(source, rows + at, put + at, BLOCK, lax.rem(late, TILES))

        behind(from_low, up_step, me, rows)
        behind(from_high, low_step, above, rows + rows * me)
        return 0

    lax.fori_loop(0, whole_steps + TILES + LAG * (n - 1), turn, 0)

    for slot in range(SLOTS):
        @pl.when(me < n - 1)
        def _():
            copy_of(*up, to_up, slot).wait_send()

        @pl.when(above < n - 1)
        def _():
            copy_of(*low, to_low, slot).wait_send()


def stream_multiply(n, steps, ident, count, pack, hidden, down_matrix, adapter_first):
    rows, depth = hidden.shape
    columns, rank = down_matrix.shape[1], adapter_first.shape[1]
    vmem = pl.BlockSpec(memory_space=pltpu.VMEM)
    anywhere = pl.BlockSpec(memory_space=pl.ANY)
    return pl.pallas_call(
        functools.partial(stream_kernel, n, steps),
        out_shape=jax.ShapeDtypeStruct((rows * n, columns + rank), jnp.bfloat16),
        in_specs=[pl.BlockSpec(memory_space=pltpu.SMEM), vmem, anywhere, anywhere, anywhere],
        out_specs=vmem,
        scratch_shapes=[
            pltpu.VMEM((rows * n, depth), jnp.bfloat16),
            pltpu.VMEM((rows * n, depth), jnp.bfloat16),
            pltpu.VMEM(down_matrix.shape, jnp.bfloat16),
            pltpu.VMEM(adapter_first.shape, jnp.bfloat16),
            pltpu.VMEM((rows, depth), jnp.bfloat16),
            pltpu.VMEM((SLOTS, CHUNK, depth), jnp.bfloat16),
            pltpu.VMEM((SLOTS, CHUNK, depth), jnp.bfloat16),
            pltpu.SemaphoreType.DMA((3,)),
            pltpu.SemaphoreType.DMA((SLOTS,)),
            pltpu.SemaphoreType.DMA((SLOTS,)),
            pltpu.SemaphoreType.DMA((steps,)),
            pltpu.SemaphoreType.DMA((steps,)),
        ],
        compiler_params=pltpu.CompilerParams(
            collective_id=ident, has_side_effects=True, vmem_limit_bytes=62 * 2**20
        ),
        cost_estimate=pl.CostEstimate(
            flops=2 * rows * n * depth * columns,
            bytes_accessed=2 * depth * columns,
            transcendentals=0,
        ),
        name=f"stream_{steps}",
    )(count, pack, hidden, down_matrix, adapter_first)


def reduce_kernel(n, terms_ref, sum_ref, from_core, from_chip, out, send_1, recv_1, send_2, recv_2):
    me = lax.axis_index("tensor")
    core = lax.rem(me, 2)
    chip = lax.div(me, 2)
    chips = n // 2
    mate = me + 1 - 2 * core
    rows = sum_ref.shape[0]

    barrier = pltpu.get_barrier_semaphore()
    pl.semaphore_signal(barrier, inc=1, device_id={"tensor": mate}, device_id_type=MESH)
    for far in range(1, chips):
        there = lax.rem(chip + far, chips) * 2 + core
        pl.semaphore_signal(barrier, inc=1, device_id={"tensor": there}, device_id_type=MESH)
    pl.semaphore_wait(barrier, chips)

    swaps = []
    for far in [*range(1, chips), 0]:
        owner_chip = lax.rem(chip + far, chips)
        swap = pltpu.make_async_remote_copy(
            src_ref=terms_ref.at[owner_chip * 2 + 1 - core],
            dst_ref=from_core.at[far],
            send_sem=send_1.at[far],
            recv_sem=recv_1.at[far],
            device_id={"tensor": mate},
            device_id_type=MESH,
        )
        swap.start()
        swaps.append((far, owner_chip, swap))

    moves = []
    for far, owner_chip, swap in swaps:
        swap.wait_recv()
        mine = owner_chip * 2 + core

        def both(i, mine=mine, far=far):
            lines = pl.ds(pl.multiple_of(i * 16, 16), 16)
            term = terms_ref[mine, lines, :].astype(jnp.float32)
            return lines, term + from_core[far, lines, :].astype(jnp.float32)

        if far > 0:
            def lines_out(i, _, both=both, far=far):
                lines, total = both(i)
                out[far - 1, lines, :] = total.astype(out.dtype)
                return 0

            lax.fori_loop(0, rows // 16, lines_out, 0)
            move = pltpu.make_async_remote_copy(
                src_ref=out.at[far - 1],
                dst_ref=from_chip.at[far - 1],
                send_sem=send_2.at[far - 1],
                recv_sem=recv_2.at[far - 1],
                device_id={"tensor": mine},
                device_id_type=MESH,
            )
            move.start()
            moves.append(move)
        else:
            def lines_own(i, _, both=both):
                lines, total = both(i)
                sum_ref[lines, :] = total
                return 0

            lax.fori_loop(0, rows // 16, lines_own, 0)

    for far, move in enumerate(moves):
        move.wait_recv()

        def lines_in(i, _, far=far):
            lines = pl.ds(pl.multiple_of(i * 16, 16), 16)
            sum_ref[lines, :] += from_chip[far, lines, :].astype(jnp.float32)
            return 0

        lax.fori_loop(0, rows // 16, lines_in, 0)

    for _, _, swap in swaps:
        swap.wait_send()
    for move in moves:
        move.wait_send()


def reduce_blocks(n, ident, terms):
    chips = n // 2
    block = terms.shape[1:]
    vmem = pl.BlockSpec(memory_space=pltpu.VMEM)
    return pl.pallas_call(
        functools.partial(reduce_kernel, n),
        out_shape=jax.ShapeDtypeStruct(block, jnp.float32),
        in_specs=[vmem],
        out_specs=vmem,
        scratch_shapes=[
            pltpu.VMEM((chips, *block), jnp.bfloat16),
            pltpu.VMEM((chips - 1, *block), jnp.bfloat16),
            pltpu.VMEM((chips - 1, *block), jnp.bfloat16),
            pltpu.SemaphoreType.DMA((chips,)),
            pltpu.SemaphoreType.DMA((chips,)),
            pltpu.SemaphoreType.DMA((chips - 1,)),
            pltpu.SemaphoreType.DMA((chips - 1,)),
        ],
        compiler_params=pltpu.CompilerParams(
            collective_id=ident, has_side_effects=True, vmem_limit_bytes=40 * 2**20
        ),
        name="reduce_blocks",
    )(terms)


def total_kernel(n_dp, n_tensor, part_ref, total_ref, held, send, recv):
    everyone = n_dp * n_tensor
    me = lax.axis_index("dp") * n_tensor + lax.axis_index("tensor")

    def device(far):
        at = lax.rem(me + far, everyone)
        return {"dp": lax.div(at, n_tensor), "tensor": lax.rem(at, n_tensor)}

    barrier = pltpu.get_barrier_semaphore()

    def greet(far, _):
        pl.semaphore_signal(barrier, inc=1, device_id=device(far), device_id_type=MESH)
        return 0

    lax.fori_loop(1, everyone, greet, 0)
    held[me] = part_ref[...]
    pl.semaphore_wait(barrier, everyone - 1)

    def copy(far, slot):
        return pltpu.make_async_remote_copy(
            src_ref=part_ref,
            dst_ref=held.at[slot],
            send_sem=send.at[far],
            recv_sem=recv.at[slot],
            device_id=device(far),
            device_id_type=MESH,
        )

    def start(far, _):
        copy(far, me).start()
        return 0

    def arrive(far, _):
        copy(far, lax.rem(me + far, everyone)).wait_recv()
        return 0

    def leave(far, _):
        copy(far, me).wait_send()
        return 0

    lax.fori_loop(1, everyone, start, 0)
    lax.fori_loop(1, everyone, arrive, 0)
    total_ref[...] = lax.fori_loop(
        0, everyone, lambda i, total: total + held[i], jnp.zeros(total_ref.shape, total_ref.dtype)
    )
    lax.fori_loop(1, everyone, leave, 0)


def total_of(n_dp, n_tensor, ident, values):
    everyone = n_dp * n_tensor
    lanes = -(-values.shape[0] // 128) * 128
    padded = jnp.zeros((8, lanes), jnp.float32).at[0, : values.shape[0]].set(values)
    vmem = pl.BlockSpec(memory_space=pltpu.VMEM)
    total = pl.pallas_call(
        functools.partial(total_kernel, n_dp, n_tensor),
        out_shape=jax.ShapeDtypeStruct(padded.shape, jnp.float32),
        in_specs=[vmem],
        out_specs=vmem,
        scratch_shapes=[
            pltpu.VMEM((everyone, *padded.shape), jnp.float32),
            pltpu.SemaphoreType.DMA((everyone,)),
            pltpu.SemaphoreType.DMA((everyone,)),
        ],
        compiler_params=pltpu.CompilerParams(collective_id=ident, has_side_effects=True),
        name="total_scores",
    )(padded)
    return total[0, : values.shape[0]]


def body(hidden, down_matrix, adapter_first, adapter_second, scoring_matrix, lengths, group_labels):
    n_tensor = lax.axis_size("tensor")
    tp_index = lax.axis_index("tensor")
    n = lax.axis_size("dp")
    me = lax.axis_index("dp")
    rows = hidden.shape[0]
    output_columns = down_matrix.shape[1]
    all_rows = rows * n
    row_block = all_rows // n_tensor
    n_seqs = lengths.shape[0]
    slot_rows = all_rows // n_seqs
    seqs_block = row_block // slot_rows
    own_seqs = rows // slot_rows

    by_source = lengths.reshape(n, own_seqs)
    counts = by_source.sum(axis=1)
    before_seq = (jnp.cumsum(by_source, axis=1) - by_source).reshape(n_seqs)
    in_slot = jnp.arange(all_rows, dtype=jnp.int32) % slot_rows
    token_valid = in_slot < jnp.repeat(lengths, slot_rows)
    place_in_source = jnp.repeat(before_seq, slot_rows) + in_slot

    own_place = lax.dynamic_slice_in_dim(place_in_source, me * rows, rows, 0)
    own_valid = lax.dynamic_slice_in_dim(token_valid, me * rows, rows, 0)
    line = jnp.arange(rows, dtype=jnp.int32)[:, None]
    pack = ((own_place[None, :] == line) & own_valid[None, :]).astype(jnp.bfloat16)
    own_count = lax.dynamic_slice_in_dim(counts, me, 1, 0)

    longest = jnp.maximum(counts[:-1].sum(), counts[1:].sum())
    longest = lax.pmax(longest, "groups")
    full = rows * (n - 1) // CHUNK
    choices = sorted({-(-full * part // 24) * 2 for part in (7, 8, 9, 10, 12)})
    limits = jnp.array([c * CHUNK for c in choices[:-1]], jnp.int32)
    chosen = (longest > limits).sum().astype(jnp.int32)
    parts = lax.switch(
        chosen,
        [functools.partial(stream_multiply, n, c, i) for i, c in enumerate(choices)],
        own_count, pack, hidden, down_matrix, adapter_first,
    )

    total = jnp.cumsum(counts)
    source = jnp.arange(n, dtype=jnp.int32)
    start = total - counts
    from_low = start[me] - total
    from_high = start - total[me]
    base_row = jnp.where(
        source == me, 0, jnp.where(source < me, rows + from_low, rows + rows * me + from_high)
    )
    token_row = jnp.repeat(base_row, rows) + place_in_source
    spread = (
        (token_row[:, None] == jnp.arange(all_rows, dtype=jnp.int32)[None, :])
        & token_valid[:, None]
    ).astype(jnp.bfloat16)
    terms = jnp.dot(spread, parts, preferred_element_type=jnp.float32).astype(jnp.bfloat16)
    summed = reduce_blocks(n_tensor, len(choices), terms.reshape(n_tensor, row_block, -1))

    base_sum = summed[:, :output_columns]
    rank_sum = summed[:, output_columns:]
    second_columns = lax.dynamic_slice_in_dim(
        adapter_second, me * output_columns, output_columns, 1
    ).astype(jnp.float32)
    policy_sum = base_sum + ADAPTER_SCALE * jnp.dot(
        rank_sum, second_columns, precision=lax.Precision.HIGHEST
    )
    block_lengths = lax.dynamic_slice_in_dim(lengths, tp_index * seqs_block, seqs_block, 0)
    row_lengths = jnp.repeat(block_lengths, slot_rows)
    is_valid = ((jnp.arange(row_block, dtype=jnp.int32) % slot_rows) < row_lengths)[:, None]
    policy_out = jnp.where(is_valid, policy_sum, 0.0).astype(jnp.bfloat16)
    reference_out = jnp.where(is_valid, base_sum, 0.0).astype(jnp.bfloat16)
    token_scores = (policy_out.astype(jnp.float32) * scoring_matrix[None, :]).sum(axis=1)
    seq_partial = token_scores.reshape(seqs_block, slot_rows).sum(axis=1)
    in_place = lax.dynamic_update_slice_in_dim(
        jnp.zeros((n_seqs,), jnp.float32), seq_partial, tp_index * seqs_block, 0
    )
    every_seq = total_of(n, n_tensor, len(choices) + 1, in_place)
    seq_score = every_seq / lengths.astype(jnp.float32)
    same_group = (group_labels[:, None] == group_labels[None, :]).astype(jnp.float32)
    group_mean = jnp.dot(same_group, seq_score, precision=lax.Precision.HIGHEST) / GSIZE
    return (policy_out, reference_out, seq_score - group_mean)


def solution(mesh):
    return jax.shard_map(
        body,
        mesh=mesh,
        in_specs=(
            P(("groups", "dp"), "tensor"),
            P("tensor", "dp"),
            P("tensor", None),
            P(),
            P("dp"),
            P("groups"),
            P("groups"),
        ),
        out_specs=(P(("groups", "tensor"), "dp"), P(("groups", "tensor"), "dp"), P("groups")),
        check_vma=False,
    )
```
